32 devices in a mesh: rows: 4 (over x, core), cols: 8 (over z, y).
Axes of the slice: x: 2, y: 2, z: 4, core: 2. Of those that a mesh axis runs over, the one named last changes fastest.
Arguments:
- values: float32 [256, 16, 32, 128], P(None, 'rows', 'cols'), may hold values from -6 to 6
- offsets: float32 [2, 16, 32, 128], P(None, 'rows', 'cols'), may hold values from 0 to 1
- nugget: float32 [16, 32, 128], P('rows', 'cols'), may hold values from 0.8 to 2.5
- neighbours: int32 [16, 32, 256], P('rows', 'cols'), may hold values from 0 to 65535, as said below
- length_scale: float32 [1], replicated, may hold values from 2.5 to 5
- target_tile: int32 [16384, 1], P(('rows', 'cols')), may hold values from 0 to 3; in each aligned block of 512 rows (0 to 511, 512 to 1023, ...) at most 256 rows name the same one
- target_spots: float32 [2, 16384], P(None, ('rows', 'cols')), may hold values from 0 to 1
Outputs:
- whitened: float32 [16, 32, 128, 256], P('rows', 'cols')
- cluster_terms: float32 [16, 32], P('rows', 'cols')
- predictions: float32 [16384, 256], P(('rows', 'cols'))
The draws below stay inside these ranges and needn't reach their ends.
Inputs may be any that keep to these rules, and one draw needn't show every extreme that they name: `neighbours`: each cluster's 256 entries are distinct points of other clusters whose two grid coordinates each differ from the cluster's own by at most 2. `target_tile`: at most 256 of the 512 targets of one device name the same tile, and in every draw some tile is named exactly 256 times by the targets of some device.
All inputs are finite; a program needn't handle non-finite values.
Results may differ from the reference program's by a relative error of at most 0.0052.
Values may be sent and summed in bfloat16 or wider, within the bound.
A program may use at most 256 MiB of HBM per device.

```python
import math
import jax
import jax.numpy as jnp
import numpy as np
from jax import lax

CLX = 4
BLOCK = 128
NEIGH = 256
HALO = 2
REPS = 256
TGT_DEV = 512
GX = 16
GY = 32
POINTS = 65536
ORDER = 384
TILES = 4
CAP = 256
TARGETS = 16384
SLAB = 16384
N_ROWS = 4
N_COLS = 8


def draw_neighbours(key, part):
    offset_pairs = [(along_x, second) for along_x in range(-HALO, HALO + 1) for second in range(-HALO, HALO + 1) if along_x != 0 or second != 0]
    shift_x = jnp.asarray(np.array([offset_pair[0] for offset_pair in offset_pairs], dtype=np.int32))
    shift_y = jnp.asarray(np.array([offset_pair[1] for offset_pair in offset_pairs], dtype=np.int32))
    offset_total = len(offset_pairs)
    grid_rows = jnp.arange(GX, dtype=jnp.int32)[:, None, None]
    grid_cols = jnp.arange(GY, dtype=jnp.int32)[None, :, None]
    cells_x = grid_rows + shift_x[None, None, :]
    cells_y = grid_cols + shift_y[None, None, :]
    inside = (cells_x >= 0) & (cells_x < GX) & (cells_y >= 0) & (cells_y < GY)
    scores = jax.random.randint(key, (GX, GY, offset_total, BLOCK), 0, 2 ** 18, dtype=jnp.int32)
    labels = jnp.arange(offset_total * BLOCK, dtype=jnp.int32).reshape(offset_total, BLOCK)
    scores = scores * 4096 + labels[None, None]
    scores = jnp.where(inside[..., None], scores, -1).reshape(GX, GY, offset_total * BLOCK)
    ignored, chosen = lax.top_k(scores, NEIGH)
    chosen_cell = chosen // BLOCK
    member = chosen % BLOCK
    near_x = grid_rows + jnp.take(shift_x, chosen_cell)
    near_y = grid_cols + jnp.take(shift_y, chosen_cell)
    return ((near_x * GY + near_y) * BLOCK + member).astype(jnp.int32)


def levels(key, dims, shards, least, largest):
    factor_of = 1.0
    for axis_at, shards_of in shards:
        draws = jax.random.uniform(jax.random.fold_in(jax.random.fold_in(key, 6), axis_at), (shards_of,), jnp.float32, least / len(shards), largest / len(shards))
        factor_of = factor_of * jnp.repeat(jnp.exp(draws), dims[axis_at] // shards_of).reshape((-1,) + (1,) * (len(dims) - 1 - axis_at))
    return factor_of


def deal_out(key, own, number, rows, amount, top, reach, lean):
    order = jax.random.permutation(key, amount)
    heavy_load, common = load_shares(amount, rows * top, reach, lean, True), load_shares(amount, rows * top, reach, lean, False)
    places = jnp.arange(amount)

    def named(sizes, offset_by):
        used = int((sizes > 0).sum())
        fixed = max(1, used // 4)
        shifted = fixed + (places - fixed + offset_by * (used - fixed)) % max(1, amount - fixed)
        return jnp.zeros((amount,), jnp.int32).at[order[jnp.where(places < fixed, places, shifted)]].set(jnp.asarray(sizes, jnp.int32))

    sizes = jnp.where(number % 4 == 0, named(heavy_load, number // 4), named(common, number - number // 4 - 1))
    mixed = jax.random.permutation(jax.random.fold_in(own, 3), amount)
    source_of, sink = mixed[0:amount // 2 * 2:2], mixed[1:amount // 2 * 2:2]
    slack = jnp.minimum(sizes[source_of] - 1, reach - sizes[sink]) // 2
    slack = jnp.where((source_of == order[0]) | (sink == order[0]) | (sizes[sink] == 0), 0, jnp.maximum(slack, 0))
    shifted = jax.random.randint(jax.random.fold_in(own, 4), (amount // 2,), 0, 1 << 20) % (slack + 1)
    sizes = sizes.at[source_of].add(-shifted).at[sink].add(shifted)
    items = jnp.searchsorted(jnp.cumsum(sizes), jnp.arange(rows * top), side="right").astype(jnp.int32)
    table = items.reshape(top, rows).T
    table = table[jax.random.permutation(jax.random.fold_in(own, 1), rows)]
    offset_by = jax.random.randint(jax.random.fold_in(own, 2), (rows, 1), 0, top)
    return jnp.take_along_axis(table, (jnp.arange(top)[None, :] + offset_by) % top, axis=1)


def load_shares(count, total, most, slope, full):
    portions = [(1 << 20) // math.isqrt(standing ** slope) + 1 for standing in range(1, count + 1)]
    largest = most if full else min(most, max(-(-total // count), total * portions[0] // sum(portions)))
    least = 1 if total - largest >= count - 1 else 0
    counts, spare = [largest] + [least] * (count - 1), total - largest - least * (count - 1)
    while spare > 0:
        free = [i for i in range(1, count) if counts[i] < largest] or [i for i in range(1, count) if counts[i] < most]
        pool, budget = sum([portions[i] for i in free]), spare
        for i in free:
            addition = min(most - counts[i], max(1, budget * portions[i] // pool), spare)
            counts[i] = counts[i] + addition
            spare = spare - addition
    return np.array(counts)


def scatter_about(stream_key, dims, scale, most, split=(), held_as=jnp.bfloat16):
    level = levels(stream_key, dims, split, -0.22, 0.18) if split else 1.0
    drawn = jax.random.normal(stream_key, dims, jnp.float32) * scale * level
    return jnp.minimum(jnp.maximum(drawn, -most), most).astype(held_as)


def setup_inputs(seed: int = 0) -> dict:
    key_list = jax.random.split(jax.random.key(seed), 8)
    values = scatter_about(key_list[0], (REPS, GX, GY, BLOCK), 1.0, 6.0, ((1, 4), (2, 8)), jnp.float32)
    offsets = jnp.clip(1.0 * jax.random.uniform(key_list[1], (2, GX, GY, BLOCK), jnp.float32) ** levels(key_list[1], (2, GX, GY, BLOCK), ((1, 4), (2, 8)), -0.2, 0.2), 0.0, 1.0)
    nugget = jnp.clip(jnp.exp(math.log(2.5) - 1.13943427 * jax.random.uniform(key_list[2], (GX, GY, BLOCK), jnp.float32) ** levels(key_list[2], (GX, GY, BLOCK), ((0, 4), (1, 8)), -0.2, 0.2)), 0.8, 2.5)
    neighbours = draw_neighbours(jax.random.fold_in(key_list[7], 71), 0)
    length_scale = jnp.clip(jax.random.uniform(key_list[4], (1,), jnp.float32, 2.5, 5.0), 2.5, 5.0)
    target_tile_keys = jax.random.split(jax.random.fold_in(key_list[5], 1), TARGETS // TGT_DEV)
    target_tile_turns = jax.random.permutation(jax.random.fold_in(key_list[5], 3), TARGETS // TGT_DEV)
    target_tile = jax.vmap(lambda own, number: deal_out(jax.random.fold_in(key_list[5], 2), own, number, TGT_DEV, TILES, 1, CAP, 2))(target_tile_keys, target_tile_turns).reshape((TARGETS, 1))
    target_spots = jnp.clip(1.0 * jax.random.uniform(key_list[6], (2, TARGETS), jnp.float32) ** levels(key_list[6], (2, TARGETS), ((1, 32),), -0.2, 0.2), 0.0, 1.0)
    return dict(values=values, offsets=offsets, nugget=nugget, neighbours=neighbours, length_scale=length_scale, target_tile=target_tile, target_spots=target_spots)


root_three = math.sqrt(3.0)

def matern(distances, length):
    scaled = root_three * distances / length
    return (1.0 + scaled) * jnp.exp(-scaled)

def cluster_work(point_data, reps, neigh, length):
    place_x = point_data[reps]
    place_y = point_data[reps + 1]
    noise_row = point_data[reps + 2]
    distances = jnp.sqrt((place_x[:, None] - place_x[None, :]) ** 2 + (place_y[:, None] - place_y[None, :]) ** 2)
    covariance = matern(distances, length) + jnp.diag(noise_row)
    factor = jnp.linalg.cholesky(covariance)
    white_all = jax.scipy.linalg.solve_triangular(factor, point_data[:reps].T, lower=True)
    tail_rows = white_all[neigh:]
    log_diag = jnp.log(jnp.diagonal(factor)[neigh:])
    total_count = tail_rows.shape[0] * reps
    cluster_term = -(0.5 * jnp.sum(tail_rows * tail_rows) + reps * jnp.sum(log_diag)) / total_count - 0.5 * math.log(2.0 * math.pi)
    return (tail_rows, cluster_term)

def cross_exact(target_x, target_y, point_x, point_y, weights, length, factor_scale):
    target_total = target_x.shape[0]
    point_total = point_x.shape[0]
    reps = weights.shape[1]
    target_step = math.gcd(target_total, 512)
    point_step = math.gcd(point_total, 4096)
    blocks_x = point_x.reshape(-1, point_step)
    blocks_y = point_y.reshape(-1, point_step)
    blocks_w = weights.reshape(-1, point_step, reps)

    def one_block(target_pair):
        rows_x, rows_y = target_pair

        def add_points(running, point_set):
            cols_x, cols_y, cols_w = point_set
            distances = jnp.sqrt((rows_x[:, None] - cols_x[None, :]) ** 2 + (rows_y[:, None] - cols_y[None, :]) ** 2)
            kernel_bf = matern(distances, length).astype(jnp.bfloat16)
            product = jnp.dot(kernel_bf.astype(jnp.float32), cols_w.astype(jnp.float32), precision=lax.Precision.HIGHEST)
            return (running + product, None)
        summed, ignored = lax.scan(add_points, jnp.zeros((target_step, reps), jnp.float32), (blocks_x, blocks_y, blocks_w))
        return summed * factor_scale
    mapped = lax.map(one_block, (target_x.reshape(-1, target_step), target_y.reshape(-1, target_step)))
    return mapped.reshape(target_total, reps)

def reference(values, offsets, nugget, neighbours, length_scale, target_tile, target_spots):
    length = length_scale[0]
    cell_x = jnp.arange(GX, dtype=jnp.int32).astype(jnp.float32)
    cell_y = jnp.arange(GY, dtype=jnp.int32).astype(jnp.float32)
    place_x = offsets[0] + cell_x[:, None, None]
    place_y = offsets[1] + cell_y[None, :, None]
    flat_x = place_x.reshape(-1)
    flat_y = place_y.reshape(-1)
    flat_values = values.reshape(REPS, -1)
    flat_nugget = nugget.reshape(-1)
    cluster_ids = jnp.arange(GX * GY, dtype=jnp.int32)
    own_pos = cluster_ids[:, None] * BLOCK + jnp.arange(BLOCK, dtype=jnp.int32)[None, :]
    all_pos = jnp.concatenate([neighbours.reshape(-1, NEIGH).astype(jnp.int32), own_pos], axis=1)
    group_size = 32

    def run_cluster(point_data):
        return cluster_work(point_data, REPS, NEIGH, length)

    def per_group(positions):
        point_data = jnp.concatenate([flat_values[:, positions], flat_x[positions][None], flat_y[positions][None], flat_nugget[positions][None]], axis=0)
        return jax.vmap(run_cluster, in_axes=1)(point_data)
    tails, terms = lax.map(per_group, all_pos.reshape(-1, group_size, ORDER))
    whitened = tails.reshape(GX, GY, BLOCK, REPS)
    cluster_terms = terms.reshape(GX, GY)
    weights = whitened.reshape(POINTS, REPS).astype(jnp.bfloat16)
    device_total = N_ROWS * N_COLS
    tile_ids = target_tile[:, 0].astype(jnp.int32)
    one_hot = (tile_ids[:, None] == jnp.arange(TILES, dtype=jnp.int32)[None, :]).astype(jnp.int32)
    per_device = one_hot.reshape(device_total, TGT_DEV, TILES)
    rank_in_tile = lax.optimization_barrier(jnp.sum((jnp.cumsum(per_device, axis=1) - 1) * per_device, axis=2)).reshape(-1)
    device_ids = jnp.arange(TARGETS, dtype=jnp.int32) // TGT_DEV
    slot_index = tile_ids * (device_total * CAP) + device_ids * CAP + rank_in_tile
    spot_x = (tile_ids.astype(jnp.float32) + target_spots[0]) * CLX
    spot_y = target_spots[1] * GY
    padded_x = jnp.zeros((TILES * device_total * CAP,), jnp.float32).at[slot_index].set(spot_x)
    padded_y = jnp.zeros((TILES * device_total * CAP,), jnp.float32).at[slot_index].set(spot_y)
    inv_root = 1.0 / math.sqrt(SLAB)

    def per_tile(tile_pack):
        tile_number, rows_x, rows_y = tile_pack
        start_point = tile_number * SLAB
        slab_x = lax.dynamic_slice_in_dim(flat_x, start_point, SLAB)
        slab_y = lax.dynamic_slice_in_dim(flat_y, start_point, SLAB)
        slab_w = lax.dynamic_slice_in_dim(weights, start_point, SLAB, 0)
        return cross_exact(rows_x, rows_y, slab_x, slab_y, slab_w, length, inv_root)
    padded = lax.map(per_tile, (jnp.arange(TILES, dtype=jnp.int32), padded_x.reshape(TILES, -1), padded_y.reshape(TILES, -1)))
    predictions = padded.reshape(-1, REPS)[slot_index]
    return (whitened, cluster_terms, predictions)
```

```python
import functools
import math

import jax
import jax.numpy as jnp
from jax import lax
from jax.experimental import pallas as pl
from jax.experimental.pallas import tpu as pltpu
from jax.sharding import PartitionSpec as P

HALO = 2
ROOT_THREE = math.sqrt(3.0)
LOG2E = math.log2(math.e)
LN2 = math.log(2.0)
F32 = jnp.float32
BF16 = jnp.bfloat16
NT = (((1,), (1,)), ((), ()))
NN = (((1,), (0,)), ((), ()))


def extended(block, sides, width):
    for axis, dim in sides:
        count = lax.axis_size(axis)
        forward = [(i, i + 1) for i in range(count - 1)]
        backward = [(target, source) for source, target in forward]
        low = lax.ppermute(
            lax.slice_in_dim(block, block.shape[dim] - width, None, axis=dim), axis, forward
        )
        high = lax.ppermute(lax.slice_in_dim(block, 0, width, axis=dim), axis, backward)
        block = jnp.concatenate([low, block, high], axis=dim)
    return block


def pieces(x):
    first = lax.reduce_precision(x, 8, 7)
    rest = x - first
    second = lax.reduce_precision(rest, 8, 7)
    third = rest - second
    return first.astype(BF16), second.astype(BF16), third.astype(BF16)


def halves(x):
    high = x.astype(BF16)
    return high, (x - high.astype(F32)).astype(BF16)


def dot_nt(a, b):
    a_high, a_low = halves(a)
    b_high, b_low = halves(b)
    return lax.dot_general(
        jnp.concatenate([a_high, a_high, a_low], axis=1),
        jnp.concatenate([b_high, b_low, b_high], axis=1),
        NT,
        preferred_element_type=F32,
    )


def matern_scaled(square):
    square = jnp.maximum(square, 1e-30)
    u = square * lax.rsqrt(square)
    return (1.0 + LN2 * u) * jnp.exp2(-u)


def cluster_kernel(span_y, scale_ref, table_ref, idx_ref, own_ref, geo_ref,
                   white_ref, weight_ref, term_ref,
                   mat, yn, k21, k31, k22, k32, k33, wt):
    clusters, block, reps = white_ref.shape
    neigh = idx_ref.shape[2]
    rows_all = table_ref.shape[1]
    window = (2 * HALO + 1) * block
    scale = scale_ref[0]

    def gather(c, carry):
        cx = c // span_y
        cy = c % span_y
        named = idx_ref[c]
        idx = named[0:1]
        shift = named.astype(F32)
        places = lax.broadcasted_iota(jnp.int32, (window, neigh), 0)
        picked = jnp.zeros((rows_all, neigh), F32)
        for dx in range(2 * HALO + 1):
            hot = jnp.where(places + dx * window == idx, 1.0, 0.0).astype(BF16)
            part = table_ref[cx + dx, :, pl.ds(pl.multiple_of(cy * block, block), window)]
            picked = picked + lax.dot_general(part, hot, NN, preferred_element_type=F32)
        yn[c] = picked[:reps].astype(BF16)
        geo = picked[reps:]
        own = geo_ref[c]
        px = jnp.concatenate([geo[0:1] + geo[1:2] + geo[2:3] + shift[1:2], own[0:1]], axis=1) * scale
        py = jnp.concatenate([geo[3:4] + geo[4:5] + geo[5:6] + shift[2:3], own[1:2]], axis=1) * scale
        noise = jnp.concatenate([geo[6:7] + geo[7:8] + geo[8:9], own[2:3]], axis=1)
        total = neigh + block
        both = jnp.concatenate(
            [px, py, jnp.zeros((126, total), F32)], axis=0
        )
        cols = both.T
        eye = lax.broadcasted_iota(jnp.int32, (block, block), 0) == lax.broadcasted_iota(
            jnp.int32, (block, block), 1
        )

        def cov(i, j):
            di, dj = slice(i * block, (i + 1) * block), slice(j * block, (j + 1) * block)
            dx = cols[di, 0:1] - px[:, dj]
            dy = cols[di, 1:2] - py[:, dj]
            k = matern_scaled(dx * dx + dy * dy)
            if i == j:
                k = k + jnp.where(eye, noise[:, dj], 0.0)
            return k

        mat[c] = cov(0, 0)
        k21[c] = cov(1, 0)
        k31[c] = cov(2, 0)
        k22[c] = cov(1, 1)
        k32[c] = cov(2, 1)
        k33[c] = cov(2, 2)
        return carry

    lax.fori_loop(0, clusters, gather, 0)

    def eliminate():
        step = 32
        for start in range(0, block, step):
            size = block - start
            lanes = lax.broadcasted_iota(jnp.int32, (1, block), 1)
            below = lax.broadcasted_iota(jnp.int32, (step, block), 0) + start

            def one(k, carry):
                pick = jnp.full((size, block), k, jnp.int32)
                for c in range(clusters):
                    row = mat[c, pl.ds(k, 1), :]
                    body_rows = mat[c, start:, :]
                    col = jnp.take_along_axis(body_rows, pick, axis=1, mode="promise_in_bounds")
                    pivot = jnp.take_along_axis(
                        jnp.broadcast_to(row, (8, block)), pick[:8], axis=1, mode="promise_in_bounds"
                    )[0:1]
                    inv = 1.0 / pivot
                    ratio = jnp.where(lanes == k, 1.0 + inv, row * inv)
                    top = jnp.where(below > k, col[:step], 0.0)
                    if size > step:
                        col = jnp.concatenate([top, col[step:]], axis=0)
                    else:
                        col = top
                    mat[c, start:, :] = body_rows - col * ratio
                return carry

            lax.fori_loop(start, start + step, one, 0)

    row_at = lax.broadcasted_iota(jnp.int32, (block, block), 0)
    col_at = lax.broadcasted_iota(jnp.int32, (block, block), 1)

    def inverse(c):
        m = mat[c]
        diag = jnp.sum(jnp.where(row_at == col_at, m, 0.0), axis=1, keepdims=True)
        unit = jnp.where(row_at > col_at, m, jnp.where(row_at == col_at, 1.0, 0.0))
        return unit * lax.rsqrt(diag), diag

    eliminate()

    def second(c, carry):
        w1, ignored = inverse(c)
        wt[c] = w1
        l21 = dot_nt(k21[c], w1)
        l31 = dot_nt(k31[c], w1)
        k21[c] = l21
        k31[c] = l31
        mat[c] = k22[c] - dot_nt(l21, l21)
        k32[c] = k32[c] - dot_nt(l31, l21)
        k33[c] = k33[c] - dot_nt(l31, l31)
        return carry

    lax.fori_loop(0, clusters, second, 0)
    eliminate()

    def third(c, carry):
        w2, ignored = inverse(c)
        k22[c] = w2
        l32 = dot_nt(k32[c], w2)
        k32[c] = l32
        mat[c] = k33[c] - dot_nt(l32, l32)
        return carry

    lax.fori_loop(0, clusters, third, 0)
    eliminate()

    def last(c, carry):
        w3, diag = inverse(c)
        white1 = dot_nt(yn[c, :, :block].astype(F32), wt[c])
        white2 = dot_nt(yn[c, :, block:].astype(F32) - dot_nt(white1, k21[c]), k22[c])
        left = (
            own_ref[:, pl.ds(pl.multiple_of(c * block, block), block)]
            - dot_nt(white1, k31[c])
            - dot_nt(white2, k32[c])
        )
        white = dot_nt(w3, left)
        white_ref[c] = white
        weight_ref[c] = white.astype(BF16)
        squares = jnp.sum(jnp.sum(white * white, axis=1, keepdims=True), axis=0, keepdims=True)
        logs = jnp.sum(jnp.log(diag), axis=0, keepdims=True)
        term = -(0.5 * squares + (0.5 * reps) * logs) / (block * reps) - 0.5 * math.log(
            2.0 * math.pi
        )
        term_ref[c] = jnp.broadcast_to(term, (8, 128))
        return carry

    lax.fori_loop(0, clusters, last, 0)


def cross_kernel(tile_rows, chunk, bounds_ref, lhs_ref, rhs_ref, weight_ref, out_ref):
    tiles, points, reps = weight_ref.shape
    out_ref[...] = jnp.zeros_like(out_ref)

    def one_tile(g, carry):
        low = bounds_ref[g]
        high = bounds_ref[g + 1]

        def one_block(b, inner):
            rows = pl.ds(pl.multiple_of(b * tile_rows, tile_rows), tile_rows)
            lhs = lhs_ref[rows, :]
            total = jnp.zeros((tile_rows, reps), F32)
            for p in range(0, points, chunk):
                square = lax.dot_general(
                    lhs, rhs_ref[g, :, p:p + chunk], NN, preferred_element_type=F32
                )
                kern = matern_scaled(square).astype(BF16)
                total = total + lax.dot_general(
                    kern, weight_ref[g, p:p + chunk, :], NN, preferred_element_type=F32
                )
            at = lax.broadcasted_iota(jnp.int32, (tile_rows, 1), 0) + b * tile_rows
            out_ref[rows, :] += jnp.where((at >= low) & (at < high), total, 0.0)
            return inner

        first = low // tile_rows
        final = jnp.where(high > low, (high + tile_rows - 1) // tile_rows, first)
        lax.fori_loop(first, final, one_block, 0)
        return carry

    lax.fori_loop(0, tiles, one_tile, 0)


def body(values, offsets, nugget, neighbours, length_scale, target_tile, target_spots):
    row_index = lax.axis_index("rows")
    col_index = lax.axis_index("cols")
    row_count = lax.axis_size("rows")
    col_count = lax.axis_size("cols")
    reps, span_x, span_y, block = values.shape
    neigh = neighbours.shape[2]
    grid_y = span_y * col_count
    clusters = span_x * span_y
    scale = (ROOT_THREE * LOG2E) / length_scale[0]
    first_x = row_index * span_x
    first_y = col_index * span_y
    cell_x = jnp.arange(span_x, dtype=jnp.int32).astype(F32)
    cell_y = (jnp.arange(span_y, dtype=jnp.int32) - span_y // 2).astype(F32)
    place_x = offsets[0] + cell_x[:, None, None]
    place_y = offsets[1] + cell_y[None, :, None]

    geo = jnp.stack([*pieces(offsets[0]), *pieces(offsets[1]), *pieces(nugget)])
    geo = jnp.concatenate([geo, jnp.zeros((7,) + geo.shape[1:], BF16)])
    packed = jnp.concatenate([values.astype(BF16), geo], axis=0)
    wide = extended(packed, (("rows", 1), ("cols", 2)), HALO)
    wide_x, wide_y = span_x + 2 * HALO, span_y + 2 * HALO
    rows_all = reps + 16
    table = jnp.transpose(wide.reshape(rows_all, wide_x, wide_y * block), (1, 0, 2))

    own_gx = first_x + jnp.arange(span_x, dtype=jnp.int32)[:, None, None]
    own_gy = first_y + jnp.arange(span_y, dtype=jnp.int32)[None, :, None]
    shift_x = neighbours // (grid_y * block) - own_gx
    shift_y = neighbours // block % grid_y - own_gy
    window = (2 * HALO + 1) * block
    idx = (shift_x + HALO) * window + (shift_y + HALO) * block + neighbours % block
    idx = jnp.stack([idx, shift_x, shift_y], axis=2).reshape(clusters, 3, neigh)
    own_geo = jnp.stack([offsets[0], offsets[1], nugget]).reshape(3, clusters, block)
    own_geo = jnp.transpose(own_geo, (1, 0, 2))
    own_geo = jnp.concatenate(
        [own_geo, jnp.zeros((clusters, 5, block), F32)], axis=1
    )

    vmem = pl.BlockSpec(memory_space=pltpu.VMEM)
    smem = pl.BlockSpec(memory_space=pltpu.SMEM)
    big = pltpu.CompilerParams(vmem_limit_bytes=56 * 1024 * 1024)
    square = pltpu.VMEM((clusters, block, block), F32)
    white, weights, terms = pl.pallas_call(
        functools.partial(cluster_kernel, span_y),
        out_shape=[
            jax.ShapeDtypeStruct((clusters, block, reps), F32),
            jax.ShapeDtypeStruct((clusters, block, reps), BF16),
            jax.ShapeDtypeStruct((clusters, 8, 128), F32),
        ],
        in_specs=[smem, vmem, vmem, vmem, vmem],
        out_specs=[vmem, vmem, vmem],
        scratch_shapes=[
            square,
            pltpu.VMEM((clusters, reps, neigh), BF16),
            square, square, square, square, square, square,
        ],
        compiler_params=big,
        name="cluster_solve",
    )(scale.reshape(1), table, idx, values.reshape(reps, clusters * block), own_geo)
    tails = white.reshape(span_x, span_y, block, reps)
    cluster_terms = terms[:, 0, 0].reshape(span_x, span_y)

    tgt_count = target_tile.shape[0]
    mine = jnp.concatenate([target_tile[:, 0].astype(F32)[None], target_spots], axis=0)
    everyone = lax.all_gather(mine, "cols", axis=1, tiled=True)
    count = tgt_count * col_count
    tile_of = everyone[0].astype(jnp.int32)
    one_hot = (tile_of[None, :] == jnp.arange(row_count, dtype=jnp.int32)[:, None]).astype(jnp.int32)
    before = jnp.cumsum(one_hot, axis=1)
    sizes = before[:, -1]
    starts = jnp.concatenate([jnp.zeros((1,), jnp.int32), jnp.cumsum(sizes)])
    position = jnp.sum((before - 1 + starts[:-1, None]) * one_hot, axis=0)
    hot = position[None, :] == jnp.arange(count, dtype=jnp.int32)[:, None]
    sorted_x = jnp.sum(jnp.where(hot, everyone[1][None, :], 0.0), axis=1)
    sorted_y = jnp.sum(jnp.where(hot, everyone[2][None, :], 0.0), axis=1)
    tx = sorted_x * span_x * scale
    ty = (sorted_y * grid_y - (first_y + span_y // 2).astype(F32)) * scale
    tx1, tx2, tx3 = pieces(-2.0 * tx)
    ty1, ty2, ty3 = pieces(-2.0 * ty)
    ones = jnp.ones((count,), BF16)
    lhs = jnp.stack(
        [tx1, tx1, tx1, tx2, tx2, tx3, ty1, ty1, ty1, ty2, ty2, ty3,
         *pieces(tx * tx + ty * ty), ones, ones, ones], axis=1
    )
    features = 32
    lhs = jnp.pad(lhs, ((0, 0), (0, features - lhs.shape[1])))
    px = (place_x * scale).reshape(-1)
    py = (place_y * scale).reshape(-1)
    px1, px2, px3 = pieces(px)
    py1, py2, py3 = pieces(py)
    unit = jnp.ones((px.shape[0],), BF16)
    rhs = jnp.stack(
        [px1, px2, px3, px1, px2, px1, py1, py2, py3, py1, py2, py1,
         unit, unit, unit, *pieces(px * px + py * py)], axis=0
    )
    rhs = jnp.pad(rhs, ((0, features - rhs.shape[0]), (0, 0)))
    all_rhs = lax.all_gather(rhs, "rows", axis=0)
    all_weights = lax.all_gather(weights.reshape(-1, reps), "rows", axis=0)
    summed = pl.pallas_call(
        functools.partial(cross_kernel, 256, 512),
        out_shape=jax.ShapeDtypeStruct((count, reps), F32),
        in_specs=[smem, vmem, vmem, vmem],
        out_specs=vmem,
        compiler_params=big,
        name="cross_sum",
    )(starts, lhs, all_rhs, all_weights)
    inv_root = 1.0 / math.sqrt(span_x * grid_y * block)
    ordered = jnp.take(summed, position, axis=0) * inv_root
    predictions = lax.psum_scatter(ordered, "cols", scatter_dimension=0, tiled=True)
    return (tails, cluster_terms, predictions)


def solution(mesh):
    return jax.shard_map(
        body,
        mesh=mesh,
        in_specs=(
            P(None, "rows", "cols", None),
            P(None, "rows", "cols", None),
            P("rows", "cols", None),
            P("rows", "cols", None),
            P(),
            P(("rows", "cols"), None),
            P(None, ("rows", "cols")),
        ),
        out_specs=(P("rows", "cols", None, None), P("rows", "cols"), P(("rows", "cols"), None)),
        check_vma=False,
    )
```

```python
import functools
import math

import jax
import jax.numpy as jnp
from jax import lax
from jax.experimental import pallas as pl
from jax.experimental.pallas import tpu as pltpu
from jax.sharding import PartitionSpec as P

HALO = 2
ROOT_THREE = math.sqrt(3.0)
LOG2E = math.log2(math.e)
LN2 = math.log(2.0)
F32 = jnp.float32
BF16 = jnp.bfloat16
NT = (((1,), (1,)), ((), ()))
NN = (((1,), (0,)), ((), ()))


def extended(block, sides, width):
    for axis, dim in sides:
        count = lax.axis_size(axis)
        forward = [(i, i + 1) for i in range(count - 1)]
        backward = [(target, source) for source, target in forward]
        low = lax.ppermute(
            lax.slice_in_dim(block, block.shape[dim] - width, None, axis=dim), axis, forward
        )
        high = lax.ppermute(lax.slice_in_dim(block, 0, width, axis=dim), axis, backward)
        block = jnp.concatenate([low, block, high], axis=dim)
    return block


def pieces(x):
    first = lax.reduce_precision(x, 8, 7)
    rest = x - first
    second = lax.reduce_precision(rest, 8, 7)
    third = rest - second
    return first.astype(BF16), second.astype(BF16), third.astype(BF16)


def halves(x):
    high = x.astype(BF16)
    return high, (x - high.astype(F32)).astype(BF16)


def dot_nt(a, b):
    a_high, a_low = halves(a)
    b_high, b_low = halves(b)
    return lax.dot_general(
        jnp.concatenate([a_high, a_high, a_low], axis=1),
        jnp.concatenate([b_high, b_low, b_high], axis=1),
        NT,
        preferred_element_type=F32,
    )


def dot_nn(a, b):
    a_high, a_low = halves(a)
    b_high, b_low = halves(b)
    return lax.dot_general(
        jnp.concatenate([a_high, a_high, a_low], axis=1),
        jnp.concatenate([b_high, b_low, b_high], axis=0),
        NN,
        preferred_element_type=F32,
    )


def matern_scaled(square):
    square = jnp.maximum(square, 1e-30)
    u = square * lax.rsqrt(square)
    return (1.0 + LN2 * u) * jnp.exp2(-u)


def cluster_kernel(span_y, scale_ref, table_ref, idx_ref, own_ref, geo_ref,
                   white_ref, weight_ref, term_ref,
                   mat, yn, k21, k31, k22, k32, k33, wt):
    clusters, block, reps = white_ref.shape
    neigh = idx_ref.shape[2]
    rows_all = table_ref.shape[1]
    window = (2 * HALO + 1) * block
    scale = scale_ref[0]

    def gather(c):
        cx = c // span_y
        cy = c % span_y
        named = idx_ref[c]
        idx = named[0:1]
        shift = named.astype(F32)
        places = lax.broadcasted_iota(jnp.int32, (window, neigh), 0)
        picked = jnp.zeros((rows_all, neigh), F32)
        for dx in range(2 * HALO + 1):
            hot = jnp.where(places + dx * window == idx, 1.0, 0.0).astype(BF16)
            part = table_ref[cx + dx, :, pl.ds(pl.multiple_of(cy * block, block), window)]
            picked = picked + lax.dot_general(part, hot, NN, preferred_element_type=F32)
        geo = picked[reps:]
        own = geo_ref[c]
        px = jnp.concatenate([geo[0:1] + geo[1:2] + geo[2:3] + shift[1:2], own[0:1]], axis=1) * scale
        py = jnp.concatenate([geo[3:4] + geo[4:5] + geo[5:6] + shift[2:3], own[1:2]], axis=1) * scale
        noise = jnp.concatenate([geo[6:7] + geo[7:8] + geo[8:9], own[2:3]], axis=1)
        total = neigh + block
        both = jnp.concatenate(
            [px, py, jnp.zeros((126, total), F32)], axis=0
        )
        cols = both.T
        eye = lax.broadcasted_iota(jnp.int32, (block, block), 0) == lax.broadcasted_iota(
            jnp.int32, (block, block), 1
        )

        def cov(i, j):
            di, dj = slice(i * block, (i + 1) * block), slice(j * block, (j + 1) * block)
            dx = cols[di, 0:1] - px[:, dj]
            dy = cols[di, 1:2] - py[:, dj]
            k = matern_scaled(dx * dx + dy * dy)
            if i == j:
                k = k + jnp.where(eye, noise[:, dj], 0.0)
            return k

        return (picked[:reps].astype(BF16), cov(0, 0), cov(1, 0), cov(2, 0), cov(1, 1),
                cov(2, 1), cov(2, 2))

    def gather_two(i, carry):
        for c, found in [(c, gather(c)) for c in (2 * i, 2 * i + 1)]:
            yn[c], mat[c], k21[c], k31[c], k22[c], k32[c], k33[c] = found
        return carry

    lax.fori_loop(0, clusters // 2, gather_two, 0)

    small = 32
    pack = block // small

    def block_inverse(packed):
        inside = lax.broadcasted_iota(jnp.int32, (1, block), 1) % small
        base = lax.broadcasted_iota(jnp.int32, (small, block), 1) // small * small
        sub = lax.broadcasted_iota(jnp.int32, (8, block), 0)
        for k in range(small):
            low = k // 8 * 8
            at = k - low
            pick = (base + k)[low:]
            done = []
            for whole in packed:
                rest = whole[low:]
                col = jnp.take_along_axis(rest, pick, axis=1, mode="promise_in_bounds")
                inv = 1.0 / col[at:at + 1]
                ratio = jnp.where(inside == k, 1.0 + inv, rest[at:at + 1] * inv)
                top = rest[:8] - jnp.where(sub > at, col[:8], 0.0) * ratio
                parts = [top] if low + 8 == small else [top, rest[8:] - col[8:] * ratio]
                if low:
                    parts = [whole[:low]] + parts
                done.append(jnp.concatenate(parts, axis=0) if len(parts) > 1 else parts[0])
            packed = done
        return packed

    def eliminate():
        r_at = lax.broadcasted_iota(jnp.int32, (small, small), 0)
        c_at = lax.broadcasted_iota(jnp.int32, (small, small), 1)
        lanes = lax.broadcasted_iota(jnp.int32, (1, block), 1)
        for start in range(0, block, small):
            end = start + small
            packed = [
                jnp.concatenate(
                    [mat[c + i, start:end, start:end] for i in range(pack)], axis=1
                )
                for c in range(0, clusters, pack)
            ]
            packed = block_inverse(packed)
            inner = (lanes >= start) & (lanes < end)
            here = lax.broadcasted_iota(jnp.int32, (small, block), 0) + start == lanes
            for c in range(clusters):
                m = packed[c // pack][:, c % pack * small:(c % pack + 1) * small]
                diag = jnp.sum(jnp.where(r_at == c_at, m, 0.0), axis=1, keepdims=True)
                unit = jnp.where(r_at > c_at, m, jnp.where(r_at == c_at, 1.0, 0.0))
                w = unit * lax.rsqrt(diag)
                rows = mat[c, start:end, :]
                rows = jnp.where(inner, jnp.where(here, 1.0, 0.0), rows)
                upper = dot_nn(w, rows)
                mat[c, start:end, :] = upper
                if end < block:
                    rest = mat[c, end:, :]
                    left = dot_nt(rest[:, start:end], w)
                    mat[c, end:, :] = jnp.where(inner, 0.0, rest) - dot_nn(left, upper)

    row_at = lax.broadcasted_iota(jnp.int32, (block, block), 0)
    col_at = lax.broadcasted_iota(jnp.int32, (block, block), 1)
    lower = row_at // small >= col_at // small
    group = 4

    def inverse(c):
        return jnp.where(lower, mat[c], 0.0)

    def grouped(work):
        def some(i, carry):
            cs = [i * group + j for j in range(group)]
            work(cs)
            return carry

        lax.fori_loop(0, clusters // group, some, 0)

    eliminate()

    def second(cs):
        w1 = [inverse(c) for c in cs]
        old = [(k21[c], k31[c], k22[c], k32[c], k33[c]) for c in cs]
        l21 = [dot_nt(o[0], w) for o, w in zip(old, w1)]
        l31 = [dot_nt(o[1], w) for o, w in zip(old, w1)]
        s22 = [o[2] - dot_nt(l, l) for o, l in zip(old, l21)]
        s32 = [o[3] - dot_nt(m, l) for o, l, m in zip(old, l21, l31)]
        s33 = [o[4] - dot_nt(m, m) for o, m in zip(old, l31)]
        for j, c in enumerate(cs):
            wt[c], k21[c], k31[c] = w1[j], l21[j], l31[j]
            mat[c], k32[c], k33[c] = s22[j], s32[j], s33[j]

    grouped(second)
    eliminate()

    def third(cs):
        w2 = [inverse(c) for c in cs]
        old = [(k32[c], k33[c]) for c in cs]
        l32 = [dot_nt(o[0], w) for o, w in zip(old, w2)]
        s33 = [o[1] - dot_nt(l, l) for o, l in zip(old, l32)]
        for j, c in enumerate(cs):
            k22[c], k32[c], mat[c] = w2[j], l32[j], s33[j]

    grouped(third)
    eliminate()

    def last(cs):
        w3 = [inverse(c) for c in cs]
        w1 = [wt[c] for c in cs]
        w2 = [k22[c] for c in cs]
        l21 = [k21[c] for c in cs]
        l31 = [k31[c] for c in cs]
        l32 = [k32[c] for c in cs]
        y1 = [yn[c, :, :block].astype(F32) for c in cs]
        y2 = [yn[c, :, block:].astype(F32) for c in cs]
        y3 = [own_ref[:, pl.ds(pl.multiple_of(c * block, block), block)] for c in cs]
        white1 = [dot_nt(y, w) for y, w in zip(y1, w1)]
        mid = [y - dot_nt(w, l) for y, w, l in zip(y2, white1, l21)]
        white2 = [dot_nt(m, w) for m, w in zip(mid, w2)]
        left = [
            y - dot_nt(jnp.concatenate([a, b], axis=1), jnp.concatenate([l, m], axis=1))
            for y, a, b, l, m in zip(y3, white1, white2, l31, l32)
        ]
        white = [dot_nt(w, y) for w, y in zip(w3, left)]
        for j, c in enumerate(cs):
            white_ref[c] = white[j]
            weight_ref[c] = white[j].astype(BF16)
            squares = jnp.sum(
                jnp.sum(white[j] * white[j], axis=1, keepdims=True), axis=0, keepdims=True
            )
            diag = jnp.sum(jnp.where(row_at == col_at, w3[j], 0.0), axis=1, keepdims=True)
            logs = -jnp.sum(jnp.log(diag), axis=0, keepdims=True)
            term = -(0.5 * squares + reps * logs) / (block * reps) - 0.5 * math.log(2.0 * math.pi)
            term_ref[c] = jnp.broadcast_to(term, (8, 128))

    grouped(last)


def cross_kernel(tile_rows, chunk, factor, bounds_ref, lhs_ref, rhs_ref, weight_ref, out_ref, acc):
    tiles, points, reps = weight_ref.shape
    sources, per, ignored = out_ref.shape
    acc[...] = jnp.zeros_like(acc)

    def one_pair(i, carry):
        g = i // sources
        source = i % sources
        low = bounds_ref[source, g]
        high = bounds_ref[source, g + 1]
        first = low // 16 * 16

        def one_block(b, inner):
            local = first + b * tile_rows
            rows = pl.ds(pl.multiple_of(source * per + local, 16), tile_rows)
            lhs = lhs_ref[rows, :]
            total = jnp.zeros((tile_rows, reps), F32)
            for p in range(0, points, chunk):
                square = lax.dot_general(
                    lhs, rhs_ref[g, :, p:p + chunk], NN, preferred_element_type=F32
                )
                kern = matern_scaled(square).astype(BF16)
                total = total + lax.dot_general(
                    kern, weight_ref[g, p:p + chunk, :], NN, preferred_element_type=F32
                )
            at = lax.broadcasted_iota(jnp.int32, (tile_rows, 1), 0) + local
            acc[rows, :] += jnp.where((at >= low) & (at < high), total, 0.0)
            return inner

        blocks = jnp.where(high > low, (high - first + tile_rows - 1) // tile_rows, 0)
        lax.fori_loop(0, blocks, one_block, 0)
        return carry

    lax.fori_loop(0, tiles * sources, one_pair, 0)

    def finish(source, carry):
        rows = pl.ds(pl.multiple_of(source * per, per), per)
        out_ref[source] = (acc[rows, :] * factor).astype(BF16)
        return carry

    lax.fori_loop(0, sources, finish, 0)


def body(values, offsets, nugget, neighbours, length_scale, target_tile, target_spots):
    row_index = lax.axis_index("rows")
    col_index = lax.axis_index("cols")
    row_count = lax.axis_size("rows")
    col_count = lax.axis_size("cols")
    reps, span_x, span_y, block = values.shape
    neigh = neighbours.shape[2]
    grid_y = span_y * col_count
    clusters = span_x * span_y
    scale = (ROOT_THREE * LOG2E) / length_scale[0]
    first_x = row_index * span_x
    first_y = col_index * span_y
    cell_x = jnp.arange(span_x, dtype=jnp.int32).astype(F32)
    cell_y = (jnp.arange(span_y, dtype=jnp.int32) - span_y // 2).astype(F32)
    place_x = offsets[0] + cell_x[:, None, None]
    place_y = offsets[1] + cell_y[None, :, None]

    geo = jnp.stack([*pieces(offsets[0]), *pieces(offsets[1]), *pieces(nugget)])
    geo = jnp.concatenate([geo, jnp.zeros((7,) + geo.shape[1:], BF16)])
    packed = jnp.concatenate([values.astype(BF16), geo], axis=0)
    wide = extended(packed, (("cols", 2),), HALO)
    target_tile, target_spots, wide = lax.optimization_barrier((target_tile, target_spots, wide))
    wide = extended(wide, (("rows", 1),), HALO)
    wide_x, wide_y = span_x + 2 * HALO, span_y + 2 * HALO
    rows_all = reps + 16
    table = jnp.transpose(wide.reshape(rows_all, wide_x, wide_y * block), (1, 0, 2))

    own_gx = first_x + jnp.arange(span_x, dtype=jnp.int32)[:, None, None]
    own_gy = first_y + jnp.arange(span_y, dtype=jnp.int32)[None, :, None]
    shift_x = neighbours // (grid_y * block) - own_gx
    shift_y = neighbours // block % grid_y - own_gy
    window = (2 * HALO + 1) * block
    idx = (shift_x + HALO) * window + (shift_y + HALO) * block + neighbours % block
    idx = jnp.stack([idx, shift_x, shift_y], axis=2).reshape(clusters, 3, neigh)
    own_geo = jnp.stack([offsets[0], offsets[1], nugget]).reshape(3, clusters, block)
    own_geo = jnp.transpose(own_geo, (1, 0, 2))
    own_geo = jnp.concatenate(
        [own_geo, jnp.zeros((clusters, 5, block), F32)], axis=1
    )

    vmem = pl.BlockSpec(memory_space=pltpu.VMEM)
    smem = pl.BlockSpec(memory_space=pltpu.SMEM)
    big = pltpu.CompilerParams(vmem_limit_bytes=56 * 1024 * 1024)
    square = pltpu.VMEM((clusters, block, block), F32)
    white, weights, terms = pl.pallas_call(
        functools.partial(cluster_kernel, span_y),
        out_shape=[
            jax.ShapeDtypeStruct((clusters, block, reps), F32),
            jax.ShapeDtypeStruct((clusters, block, reps), BF16),
            jax.ShapeDtypeStruct((clusters, 8, 128), F32),
        ],
        in_specs=[smem, vmem, vmem, vmem, vmem],
        out_specs=[vmem, vmem, vmem],
        scratch_shapes=[
            square,
            pltpu.VMEM((clusters, reps, neigh), BF16),
            square, square, square, square, square, square,
        ],
        compiler_params=big,
        name="cluster_solve",
    )(scale.reshape(1), table, idx, values.reshape(reps, clusters * block), own_geo)
    tails = white.reshape(span_x, span_y, block, reps)
    cluster_terms = terms[:, 0, 0].reshape(span_x, span_y)

    tgt_count = target_tile.shape[0]
    one_hot = (
        target_tile == jnp.arange(row_count, dtype=jnp.int32)[None, :]
    ).astype(jnp.int32)
    before = jnp.cumsum(one_hot, axis=0)
    starts = jnp.concatenate([jnp.zeros((1,), jnp.int32), jnp.cumsum(before[-1])])
    position = jnp.sum((before - 1 + starts[None, :-1]) * one_hot, axis=1)
    hot = (
        position[None, :] == jnp.arange(tgt_count, dtype=jnp.int32)[:, None]
    ).astype(F32)
    sorted_spots = jnp.sum(hot[None] * target_spots[:, None, :], axis=2)
    padded_starts = jnp.pad(starts.astype(F32), (0, tgt_count - row_count - 1))
    mine = jnp.concatenate([sorted_spots, padded_starts[None]], axis=0)
    everyone = lax.all_gather(mine, "cols", axis=1, tiled=True)
    bounds = everyone[2].reshape(col_count, tgt_count)[:, :row_count + 1].astype(jnp.int32)
    tile_rows = 128
    spots = jnp.pad(everyone[:2], ((0, 0), (0, tile_rows)))
    sorted_x, sorted_y = spots[0], spots[1]
    count = tgt_count * col_count + tile_rows
    tx = sorted_x * span_x * scale
    ty = (sorted_y * grid_y - (first_y + span_y // 2).astype(F32)) * scale
    tx1, tx2, tx3 = pieces(-2.0 * tx)
    ty1, ty2, ty3 = pieces(-2.0 * ty)
    ones = jnp.ones((count,), BF16)
    lhs = jnp.stack(
        [tx1, tx1, tx1, tx2, tx2, tx3, ty1, ty1, ty1, ty2, ty2, ty3,
         *pieces(tx * tx + ty * ty), ones, ones, ones], axis=1
    )
    features = 32
    lhs = jnp.pad(lhs, ((0, 0), (0, features - lhs.shape[1])))
    px = (place_x * scale).reshape(-1)
    py = (place_y * scale).reshape(-1)
    px1, px2, px3 = pieces(px)
    py1, py2, py3 = pieces(py)
    unit = jnp.ones((px.shape[0],), BF16)
    rhs = jnp.stack(
        [px1, px2, px3, px1, px2, px1, py1, py2, py3, py1, py2, py1,
         unit, unit, unit, *pieces(px * px + py * py)], axis=0
    )
    rhs = jnp.pad(rhs, ((0, features - rhs.shape[0]), (0, 0)))
    all_rhs = lax.all_gather(rhs, "rows", axis=0)
    all_weights = lax.all_gather(weights.reshape(-1, reps), "rows", axis=0)
    inv_root = 1.0 / math.sqrt(span_x * grid_y * block)
    partial = pl.pallas_call(
        functools.partial(cross_kernel, tile_rows, math.gcd(px.shape[0], 512), inv_root),
        out_shape=jax.ShapeDtypeStruct((col_count, tgt_count, reps), BF16),
        in_specs=[smem, vmem, vmem, vmem],
        out_specs=vmem,
        scratch_shapes=[pltpu.VMEM((count, reps), F32)],
        compiler_params=big,
        name="cross_sum",
    )(bounds, lhs, all_rhs, all_weights)
    arrived = lax.all_to_all(partial, "cols", split_axis=0, concat_axis=0, tiled=True)
    ordered = jnp.sum(arrived.astype(F32), axis=0)
    predictions = lax.dot_general(
        hot, ordered, (((0,), (0,)), ((), ())), precision=lax.Precision.HIGHEST
    )
    return (tails, cluster_terms, predictions)


def solution(mesh):
    return jax.shard_map(
        body,
        mesh=mesh,
        in_specs=(
            P(None, "rows", "cols", None),
            P(None, "rows", "cols", None),
            P("rows", "cols", None),
            P("rows", "cols", None),
            P(),
            P(("rows", "cols"), None),
            P(None, ("rows", "cols")),
        ),
        out_specs=(P("rows", "cols", None, None), P("rows", "cols"), P(("rows", "cols"), None)),
        check_vma=False,
    )
```

```python
import functools
import math

import jax
import jax.numpy as jnp
from jax import lax
from jax.experimental import pallas as pl
from jax.experimental.pallas import tpu as pltpu
from jax.sharding import PartitionSpec as P

HALO = 2
ROOT_THREE = math.sqrt(3.0)
LOG2E = math.log2(math.e)
LN2 = math.log(2.0)
F32 = jnp.float32
BF16 = jnp.bfloat16
NT = (((1,), (1,)), ((), ()))
NN = (((1,), (0,)), ((), ()))


def extended(block, sides, width):
    for axis, dim in sides:
        count = lax.axis_size(axis)
        forward = [(i, i + 1) for i in range(count - 1)]
        backward = [(target, source) for source, target in forward]
        low = lax.ppermute(
            lax.slice_in_dim(block, block.shape[dim] - width, None, axis=dim), axis, forward
        )
        high = lax.ppermute(lax.slice_in_dim(block, 0, width, axis=dim), axis, backward)
        block = jnp.concatenate([low, block, high], axis=dim)
    return block


def pieces(x):
    first = lax.reduce_precision(x, 8, 7)
    rest = x - first
    second = lax.reduce_precision(rest, 8, 7)
    third = rest - second
    return first.astype(BF16), second.astype(BF16), third.astype(BF16)


def halves(x):
    high = x.astype(BF16)
    return high, (x - high.astype(F32)).astype(BF16)


def dot_nt(a, b):
    a_high, a_low = halves(a)
    b_high, b_low = halves(b)
    return lax.dot_general(
        jnp.concatenate([a_high, a_high, a_low], axis=1),
        jnp.concatenate([b_high, b_low, b_high], axis=1),
        NT,
        preferred_element_type=F32,
    )


def dot_nn(a, b):
    a_high, a_low = halves(a)
    b_high, b_low = halves(b)
    return lax.dot_general(
        jnp.concatenate([a_high, a_high, a_low], axis=1),
        jnp.concatenate([b_high, b_low, b_high], axis=0),
        NN,
        preferred_element_type=F32,
    )


def matern_scaled(square):
    square = jnp.maximum(square, 1e-30)
    u = square * lax.rsqrt(square)
    return (1.0 + LN2 * u) * jnp.exp2(-u)


def cluster_kernel(span_y, scale_ref, table_ref, idx_ref, own_ref, geo_ref,
                   white_ref, weight_ref, term_ref,
                   mat, yn, k21, k31, k22, k32, k33, wt):
    clusters, block, reps = white_ref.shape
    neigh = idx_ref.shape[2]
    rows_all = table_ref.shape[1]
    window = (2 * HALO + 1) * block
    scale = scale_ref[0]

    def gather(c):
        cx = c // span_y
        cy = c % span_y
        named = idx_ref[c]
        idx = named[0:1]
        shift = named.astype(F32)
        places = lax.broadcasted_iota(jnp.int32, (window, neigh), 0)
        picked = jnp.zeros((rows_all, neigh), F32)
        for dx in range(2 * HALO + 1):
            hot = jnp.where(places + dx * window == idx, 1.0, 0.0).astype(BF16)
            part = table_ref[cx + dx, :, pl.ds(pl.multiple_of(cy * block, block), window)]
            picked = picked + lax.dot_general(part, hot, NN, preferred_element_type=F32)
        geo = picked[reps:]
        own = geo_ref[c]
        px = jnp.concatenate([geo[0:1] + geo[1:2] + geo[2:3] + shift[1:2], own[0:1]], axis=1) * scale
        py = jnp.concatenate([geo[3:4] + geo[4:5] + geo[5:6] + shift[2:3], own[1:2]], axis=1) * scale
        noise = jnp.concatenate([geo[6:7] + geo[7:8] + geo[8:9], own[2:3]], axis=1)
        total = neigh + block
        both = jnp.concatenate(
            [px, py, jnp.zeros((126, total), F32)], axis=0
        )
        cols = both.T
        eye = lax.broadcasted_iota(jnp.int32, (block, block), 0) == lax.broadcasted_iota(
            jnp.int32, (block, block), 1
        )

        def cov(i, j):
            di, dj = slice(i * block, (i + 1) * block), slice(j * block, (j + 1) * block)
            dx = cols[di, 0:1] - px[:, dj]
            dy = cols[di, 1:2] - py[:, dj]
            k = matern_scaled(dx * dx + dy * dy)
            if i == j:
                k = k + jnp.where(eye, noise[:, dj], 0.0)
            return k

        return (picked[:reps].astype(BF16), cov(0, 0), cov(1, 0), cov(2, 0), cov(1, 1),
                cov(2, 1), cov(2, 2))

    def gather_two(i, carry):
        for c, found in [(c, gather(c)) for c in (2 * i, 2 * i + 1)]:
            yn[c], mat[c], k21[c], k31[c], k22[c], k32[c], k33[c] = found
        return carry

    lax.fori_loop(0, clusters // 2, gather_two, 0)

    small = 32
    pack = block // small

    def block_inverse(packed):
        inside = lax.broadcasted_iota(jnp.int32, (1, block), 1) % small
        base = lax.broadcasted_iota(jnp.int32, (small, block), 1) // small * small
        sub = lax.broadcasted_iota(jnp.int32, (8, block), 0)
        for k in range(small):
            low = k // 8 * 8
            at = k - low
            pick = (base + k)[low:]
            done = []
            for whole in packed:
                rest = whole[low:]
                col = jnp.take_along_axis(rest, pick, axis=1, mode="promise_in_bounds")
                inv = 1.0 / col[at:at + 1]
                ratio = jnp.where(inside == k, 1.0 + inv, rest[at:at + 1] * inv)
                top = rest[:8] - jnp.where(sub > at, col[:8], 0.0) * ratio
                parts = [top] if low + 8 == small else [top, rest[8:] - col[8:] * ratio]
                if low:
                    parts = [whole[:low]] + parts
                done.append(jnp.concatenate(parts, axis=0) if len(parts) > 1 else parts[0])
            packed = done
        return packed

    def eliminate():
        r_at = lax.broadcasted_iota(jnp.int32, (small, small), 0)
        c_at = lax.broadcasted_iota(jnp.int32, (small, small), 1)
        lanes = lax.broadcasted_iota(jnp.int32, (1, block), 1)
        for start in range(0, block, small):
            end = start + small
            packed = [
                jnp.concatenate(
                    [mat[c + i, start:end, start:end] for i in range(pack)], axis=1
                )
                for c in range(0, clusters, pack)
            ]
            packed = block_inverse(packed)
            inner = (lanes >= start) & (lanes < end)
            here = lax.broadcasted_iota(jnp.int32, (small, block), 0) + start == lanes
            for c in range(clusters):
                m = packed[c // pack][:, c % pack * small:(c % pack + 1) * small]
                diag = jnp.sum(jnp.where(r_at == c_at, m, 0.0), axis=1, keepdims=True)
                unit = jnp.where(r_at > c_at, m, jnp.where(r_at == c_at, 1.0, 0.0))
                w = unit * lax.rsqrt(diag)
                rows = mat[c, start:end, :]
                rows = jnp.where(inner, jnp.where(here, 1.0, 0.0), rows)
                upper = dot_nn(w, rows)
                mat[c, start:end, :] = upper
                if end < block:
                    rest = mat[c, end:, :]
                    left = dot_nt(rest[:, start:end], w)
                    mat[c, end:, :] = jnp.where(inner, 0.0, rest) - dot_nn(left, upper)

    row_at = lax.broadcasted_iota(jnp.int32, (block, block), 0)
    col_at = lax.broadcasted_iota(jnp.int32, (block, block), 1)
    lower = row_at // small >= col_at // small
    group = 4

    def inverse(c):
        return jnp.where(lower, mat[c], 0.0)

    def grouped(work):
        def some(i, carry):
            cs = [i * group + j for j in range(group)]
            work(cs)
            return carry

        lax.fori_loop(0, clusters // group, some, 0)

    eliminate()

    def second(cs):
        w1 = [inverse(c) for c in cs]
        old = [(k21[c], k31[c], k22[c], k32[c], k33[c]) for c in cs]
        l21 = [dot_nt(o[0], w) for o, w in zip(old, w1)]
        l31 = [dot_nt(o[1], w) for o, w in zip(old, w1)]
        s22 = [o[2] - dot_nt(l, l) for o, l in zip(old, l21)]
        s32 = [o[3] - dot_nt(m, l) for o, l, m in zip(old, l21, l31)]
        s33 = [o[4] - dot_nt(m, m) for o, m in zip(old, l31)]
        for j, c in enumerate(cs):
            wt[c], k21[c], k31[c] = w1[j], l21[j], l31[j]
            mat[c], k32[c], k33[c] = s22[j], s32[j], s33[j]

    grouped(second)
    eliminate()

    def third(cs):
        w2 = [inverse(c) for c in cs]
        old = [(k32[c], k33[c]) for c in cs]
        l32 = [dot_nt(o[0], w) for o, w in zip(old, w2)]
        s33 = [o[1] - dot_nt(l, l) for o, l in zip(old, l32)]
        for j, c in enumerate(cs):
            k22[c], k32[c], mat[c] = w2[j], l32[j], s33[j]

    grouped(third)
    eliminate()

    def last(cs):
        w3 = [inverse(c) for c in cs]
        w1 = [wt[c] for c in cs]
        w2 = [k22[c] for c in cs]
        l21 = [k21[c] for c in cs]
        l31 = [k31[c] for c in cs]
        l32 = [k32[c] for c in cs]
        y1 = [yn[c, :, :block].astype(F32) for c in cs]
        y2 = [yn[c, :, block:].astype(F32) for c in cs]
        y3 = [own_ref[:, pl.ds(pl.multiple_of(c * block, block), block)] for c in cs]
        white1 = [dot_nt(y, w) for y, w in zip(y1, w1)]
        mid = [y - dot_nt(w, l) for y, w, l in zip(y2, white1, l21)]
        white2 = [dot_nt(m, w) for m, w in zip(mid, w2)]
        left = [
            y - dot_nt(jnp.concatenate([a, b], axis=1), jnp.concatenate([l, m], axis=1))
            for y, a, b, l, m in zip(y3, white1, white2, l31, l32)
        ]
        white = [dot_nt(w, y) for w, y in zip(w3, left)]
        for j, c in enumerate(cs):
            white_ref[c] = white[j]
            weight_ref[c] = white[j].astype(BF16)
            squares = jnp.sum(
                jnp.sum(white[j] * white[j], axis=1, keepdims=True), axis=0, keepdims=True
            )
            diag = jnp.sum(jnp.where(row_at == col_at, w3[j], 0.0), axis=1, keepdims=True)
            logs = -jnp.sum(jnp.log(diag), axis=0, keepdims=True)
            term = -(0.5 * squares + reps * logs) / (block * reps) - 0.5 * math.log(2.0 * math.pi)
            term_ref[c] = jnp.broadcast_to(term, (8, 128))

    grouped(last)


def cross_kernel(tile_rows, chunk, factor, bounds_ref, lhs_ref, rhs_ref, weight_ref, out_ref, acc):
    tiles, points, reps = weight_ref.shape
    sources, per, ignored = out_ref.shape
    acc[...] = jnp.zeros_like(acc)

    def one_pair(i, carry):
        g = i // sources
        source = i % sources
        low = bounds_ref[source, g]
        high = bounds_ref[source, g + 1]
        first = low // 16 * 16

        def one_block(b, inner):
            local = first + b * tile_rows
            rows = pl.ds(pl.multiple_of(source * per + local, 16), tile_rows)
            lhs = lhs_ref[rows, :]
            total = jnp.zeros((tile_rows, reps), F32)
            for p in range(0, points, chunk):
                square = lax.dot_general(
                    lhs, rhs_ref[g, :, p:p + chunk], NN, preferred_element_type=F32
                )
                kern = matern_scaled(square).astype(BF16)
                total = total + lax.dot_general(
                    kern, weight_ref[g, p:p + chunk, :], NN, preferred_element_type=F32
                )
            at = lax.broadcasted_iota(jnp.int32, (tile_rows, 1), 0) + local
            acc[rows, :] += jnp.where((at >= low) & (at < high), total, 0.0)
            return inner

        blocks = jnp.where(high > low, (high - first + tile_rows - 1) // tile_rows, 0)
        lax.fori_loop(0, blocks, one_block, 0)
        return carry

    lax.fori_loop(0, tiles * sources, one_pair, 0)

    def finish(source, carry):
        rows = pl.ds(pl.multiple_of(source * per, per), per)
        out_ref[source] = (acc[rows, :] * factor).astype(BF16)
        return carry

    lax.fori_loop(0, sources, finish, 0)


def body(values, offsets, nugget, neighbours, length_scale, target_tile, target_spots):
    row_index = lax.axis_index("rows")
    col_index = lax.axis_index("cols")
    row_count = lax.axis_size("rows")
    col_count = lax.axis_size("cols")
    reps, span_x, span_y, block = values.shape
    neigh = neighbours.shape[2]
    grid_y = span_y * col_count
    clusters = span_x * span_y
    scale = (ROOT_THREE * LOG2E) / length_scale[0]
    first_x = row_index * span_x
    first_y = col_index * span_y
    cell_x = jnp.arange(span_x, dtype=jnp.int32).astype(F32)
    cell_y = (jnp.arange(span_y, dtype=jnp.int32) - span_y // 2).astype(F32)
    place_x = offsets[0] + cell_x[:, None, None]
    place_y = offsets[1] + cell_y[None, :, None]

    geo = jnp.stack([*pieces(offsets[0]), *pieces(offsets[1]), *pieces(nugget)])
    geo = jnp.concatenate([geo, jnp.zeros((7,) + geo.shape[1:], BF16)])
    packed = jnp.concatenate([values.astype(BF16), geo], axis=0)
    wide = extended(packed, (("cols", 2),), HALO)
    wide = extended(wide, (("rows", 1),), HALO)
    wide_x, wide_y = span_x + 2 * HALO, span_y + 2 * HALO
    rows_all = reps + 16
    table = jnp.transpose(wide.reshape(rows_all, wide_x, wide_y * block), (1, 0, 2))

    tgt_count = target_tile.shape[0]
    one_hot = (
        target_tile == jnp.arange(row_count, dtype=jnp.int32)[None, :]
    ).astype(jnp.int32)
    before = jnp.cumsum(one_hot, axis=0)
    starts = jnp.concatenate([jnp.zeros((1,), jnp.int32), jnp.cumsum(before[-1])])
    position = jnp.sum((before - 1 + starts[None, :-1]) * one_hot, axis=1)
    hot = (
        position[None, :] == jnp.arange(tgt_count, dtype=jnp.int32)[:, None]
    ).astype(F32)
    sorted_spots = jnp.sum(hot[None] * target_spots[:, None, :], axis=2)
    padded_starts = jnp.pad(starts.astype(F32), (0, tgt_count - row_count - 1))
    mine = jnp.concatenate([sorted_spots, padded_starts[None]], axis=0)
    everyone = lax.all_gather(mine, "cols", axis=1, tiled=True)
    table, everyone = lax.optimization_barrier((table, everyone))

    own_gx = first_x + jnp.arange(span_x, dtype=jnp.int32)[:, None, None]
    own_gy = first_y + jnp.arange(span_y, dtype=jnp.int32)[None, :, None]
    shift_x = neighbours // (grid_y * block) - own_gx
    shift_y = neighbours // block % grid_y - own_gy
    window = (2 * HALO + 1) * block
    idx = (shift_x + HALO) * window + (shift_y + HALO) * block + neighbours % block
    idx = jnp.stack([idx, shift_x, shift_y], axis=2).reshape(clusters, 3, neigh)
    own_geo = jnp.stack([offsets[0], offsets[1], nugget]).reshape(3, clusters, block)
    own_geo = jnp.transpose(own_geo, (1, 0, 2))
    own_geo = jnp.concatenate(
        [own_geo, jnp.zeros((clusters, 5, block), F32)], axis=1
    )

    vmem = pl.BlockSpec(memory_space=pltpu.VMEM)
    smem = pl.BlockSpec(memory_space=pltpu.SMEM)
    big = pltpu.CompilerParams(vmem_limit_bytes=56 * 1024 * 1024)
    square = pltpu.VMEM((clusters, block, block), F32)
    white, weights, terms = pl.pallas_call(
        functools.partial(cluster_kernel, span_y),
        out_shape=[
            jax.ShapeDtypeStruct((clusters, block, reps), F32),
            jax.ShapeDtypeStruct((clusters, block, reps), BF16),
            jax.ShapeDtypeStruct((clusters, 8, 128), F32),
        ],
        in_specs=[smem, vmem, vmem, vmem, vmem],
        out_specs=[vmem, vmem, vmem],
        scratch_shapes=[
            square,
            pltpu.VMEM((clusters, reps, neigh), BF16),
            square, square, square, square, square, square,
        ],
        compiler_params=big,
        name="cluster_solve",
    )(scale.reshape(1), table, idx, values.reshape(reps, clusters * block), own_geo)
    tails = white.reshape(span_x, span_y, block, reps)
    cluster_terms = terms[:, 0, 0].reshape(span_x, span_y)

    bounds = everyone[2].reshape(col_count, tgt_count)[:, :row_count + 1].astype(jnp.int32)
    tile_rows = 128
    spots = jnp.pad(everyone[:2], ((0, 0), (0, tile_rows)))
    sorted_x, sorted_y = spots[0], spots[1]
    count = tgt_count * col_count + tile_rows
    tx = sorted_x * span_x * scale
    ty = (sorted_y * grid_y - (first_y + span_y // 2).astype(F32)) * scale
    tx1, tx2, tx3 = pieces(-2.0 * tx)
    ty1, ty2, ty3 = pieces(-2.0 * ty)
    ones = jnp.ones((count,), BF16)
    lhs = jnp.stack(
        [tx1, tx1, tx1, tx2, tx2, tx3, ty1, ty1, ty1, ty2, ty2, ty3,
         *pieces(tx * tx + ty * ty), ones, ones, ones], axis=1
    )
    features = 32
    lhs = jnp.pad(lhs, ((0, 0), (0, features - lhs.shape[1])))
    px = (place_x * scale).reshape(-1)
    py = (place_y * scale).reshape(-1)
    px1, px2, px3 = pieces(px)
    py1, py2, py3 = pieces(py)
    unit = jnp.ones((px.shape[0],), BF16)
    rhs = jnp.stack(
        [px1, px2, px3, px1, px2, px1, py1, py2, py3, py1, py2, py1,
         unit, unit, unit, *pieces(px * px + py * py)], axis=0
    )
    rhs = jnp.pad(rhs, ((0, features - rhs.shape[0]), (0, 0)))
    all_rhs = lax.all_gather(rhs, "rows", axis=0)
    all_weights = lax.all_gather(weights.reshape(-1, reps), "rows", axis=0)
    inv_root = 1.0 / math.sqrt(span_x * grid_y * block)
    partial = pl.pallas_call(
        functools.partial(cross_kernel, tile_rows, math.gcd(px.shape[0], 512), inv_root),
        out_shape=jax.ShapeDtypeStruct((col_count, tgt_count, reps), BF16),
        in_specs=[smem, vmem, vmem, vmem],
        out_specs=vmem,
        scratch_shapes=[pltpu.VMEM((count, reps), F32)],
        compiler_params=big,
        name="cross_sum",
    )(bounds, lhs, all_rhs, all_weights)
    arrived = lax.all_to_all(partial, "cols", split_axis=0, concat_axis=0, tiled=True)
    ordered = jnp.sum(arrived.astype(F32), axis=0)
    predictions = lax.dot_general(
        hot, ordered, (((0,), (0,)), ((), ())), precision=lax.Precision.HIGHEST
    )
    return (tails, cluster_terms, predictions)


def solution(mesh):
    return jax.shard_map(
        body,
        mesh=mesh,
        in_specs=(
            P(None, "rows", "cols", None),
            P(None, "rows", "cols", None),
            P("rows", "cols", None),
            P("rows", "cols", None),
            P(),
            P(("rows", "cols"), None),
            P(None, ("rows", "cols")),
        ),
        out_specs=(P("rows", "cols", None, None), P("rows", "cols"), P(("rows", "cols"), None)),
        check_vma=False,
    )
```
